32 devices in a mesh: shot: 16 (over z, x, core), depth: 2 (over y).
Axes of the slice: x: 2, y: 2, z: 4, core: 2. Of those that a mesh axis runs over, the one named last changes fastest.
Arguments:
- u_prev: float32 [16, 64, 32, 128], P('shot', None, 'depth'), may hold values from -8 to 8.5
- u_cur: float32 [16, 64, 32, 128], P('shot', None, 'depth'), may hold values from -8 to 8.5
- a_prev: float32 [16, 64, 32, 128], P('shot', None, 'depth'), may hold values from -8 to 8.5
- a_cur: float32 [16, 64, 32, 128], P('shot', None, 'depth'), may hold values from -8 to 8.5
- model: float32 [64, 32, 128], P('shot', 'depth'), may hold values from 0.03 to 0.09
- aniso_h: float32 [64, 32, 128], P('shot', 'depth'), may hold values from 0.7 to 1.5
- aniso_c: float32 [64, 32, 128], P('shot', 'depth'), may hold values from -0.5 to 0.5
- smooth_coef: float32 [64, 32, 128], P('shot', 'depth'), may hold values from 0.02 to 0.16
- bin_onehot: int32 [16, 4, 4], P(None, 'depth'), may hold values from 0 to 1, as said below
- shot_group: int32 [16], P('shot'), may hold values from 0 to 15
- src_cell: int32 [16], P('shot'), may hold values from 0 to 262143
- rec_cell: int32 [16, 128], P('shot'), may hold values from 0 to 262143
- src_wave: float32 [16, 3], P('shot'), may hold values from -6 to 6
- rec_data: float32 [16, 2, 128], P('shot'), may hold values from -6 to 6
Outputs:
- model_next: float32 [64, 32, 128], P('shot', 'depth')
- grad_dir: float32 [64, 32, 128], P('shot', 'depth')
- wave_next: float32 [16, 64, 32, 128], P('shot', None, 'depth')
The draws below stay inside these ranges and needn't reach their ends.
Inputs may be any that keep to these rules, and one draw needn't show every extreme that they name: `bin_onehot`: each entry along the last dimension is one-hot: exactly one 1 per row.
All inputs are finite; a program needn't handle non-finite values.
Results may differ from the reference program's by a relative error of at most 0.000092.
Values sent between devices are 32-bit elements; how exact they have to be, the bound alone decides.
A program may use at most 64 MiB of HBM per device.

```python
import math
import jax
import jax.numpy as jnp
from jax import lax

NX = 64
NY = 128
NREC = 128
STEPS = 2
GROUPS = 16
BZ = 8
NBINS = 4
NZ = 32
SHOTS = 16
NBLK = 4


def wave_field(key, salt):
    key = jax.random.fold_in(key, salt)
    along_x = jnp.arange(NX, dtype=jnp.float32) / NX
    along_z = jnp.arange(NZ, dtype=jnp.float32) / NZ
    base = jnp.clip(jax.random.normal(key, (SHOTS, NX, NZ, NY), jnp.float32), -5.0, 5.0)
    growth = jnp.exp2(0.585 * along_x)[:, None, None] * jnp.exp2(0.585 * along_z)[None, :, None]
    return 0.5 * growth * base


def draw_u_prev(key, part):
    return wave_field(key, 11)


def draw_u_cur(key, part):
    return wave_field(key, 12)


def draw_a_prev(key, part):
    return wave_field(key, 13)


def draw_a_cur(key, part):
    return wave_field(key, 14)


def draw_bin_onehot(key, part):
    chosen = jax.random.randint(jax.random.fold_in(key, 21), (GROUPS, NBLK), 0, NBINS)
    return (chosen[:, :, None] == jnp.arange(NBINS, dtype=jnp.int32)).astype(jnp.int32)


def plant(values, rng, least, high):
    extent = values.shape
    spot = [jax.random.randint(jax.random.fold_in(rng, axis), (), 0, extent[axis]) for axis in range(len(extent))]
    values = values.at[tuple(spot)].set(least)
    longest = extent.index(max(extent))
    spot[longest] = (spot[longest] + 1) % extent[longest]
    return values.at[tuple(spot)].set(high)


def block_scale(own_key, dims, pieces, low, largest):
    level = 1.0
    for dim, blocks in pieces:
        steps = jax.random.uniform(jax.random.fold_in(jax.random.fold_in(own_key, 6), dim), (blocks,), jnp.float32, low / len(pieces), largest / len(pieces))
        level = level * jnp.repeat(jnp.exp(steps), dims[dim] // blocks).reshape((-1,) + (1,) * (len(dims) - 1 - dim))
    return level


def centred(own_key, extent, deviation, bound, pieces=(), kind=jnp.bfloat16):
    level = block_scale(own_key, extent, pieces, -0.22, 0.18) if pieces else 1.0
    values = jax.random.normal(own_key, extent, jnp.float32) * deviation * level
    return jnp.minimum(jnp.maximum(values, -bound), bound).astype(kind)


def setup_inputs(seed: int = 0) -> dict:
    keys = jax.random.split(jax.random.key(seed), 15)
    return {
        "u_prev": draw_u_prev(jax.random.fold_in(keys[14], 71), 0),
        "u_cur": draw_u_cur(jax.random.fold_in(keys[14], 71), 0),
        "a_prev": draw_a_prev(jax.random.fold_in(keys[14], 71), 0),
        "a_cur": draw_a_cur(jax.random.fold_in(keys[14], 71), 0),
        "model": jnp.clip(jnp.exp(math.log(0.09) - 1.09861235 * jax.random.uniform(keys[4], (NX, NZ, NY), jnp.float32) ** block_scale(keys[4], (NX, NZ, NY), ((0, 16), (1, 2)), -0.2, 0.2)), 0.03, 0.09),
        "aniso_h": jnp.clip(jnp.exp(math.log(1.5) - 0.7621401 * jax.random.uniform(keys[5], (NX, NZ, NY), jnp.float32) ** block_scale(keys[5], (NX, NZ, NY), ((0, 16), (1, 2)), -0.2, 0.2)), 0.7, 1.5),
        "aniso_c": jnp.clip(jax.random.uniform(keys[6], (NX, NZ, NY), jnp.float32, -0.5, 0.5) * block_scale(keys[6], (NX, NZ, NY), ((0, 16), (1, 2)), -0.4, 0.0), -0.5, 0.5),
        "smooth_coef": jnp.clip(0.02 + 0.14 * jax.random.uniform(keys[7], (NX, NZ, NY), jnp.float32) ** block_scale(keys[7], (NX, NZ, NY), ((0, 16), (1, 2)), -0.2, 0.2), 0.02, 0.16),
        "bin_onehot": draw_bin_onehot(jax.random.fold_in(keys[14], 71), 0),
        "shot_group": plant(jax.random.randint(keys[9], (SHOTS,), 0, GROUPS), jax.random.fold_in(keys[9], 1), 0, GROUPS - 1).astype(jnp.int32),
        "src_cell": plant(jax.random.randint(keys[10], (SHOTS,), 0, NX * NZ * NY), jax.random.fold_in(keys[10], 1), 0, (NX * NZ * NY) - 1).astype(jnp.int32),
        "rec_cell": plant(jax.random.randint(keys[11], (SHOTS, NREC), 0, NX * NZ * NY), jax.random.fold_in(keys[11], 1), 0, (NX * NZ * NY) - 1).astype(jnp.int32),
        "src_wave": centred(keys[12], (SHOTS, STEPS + 1), 1.0, 6.0, ((0, 16),), jnp.float32),
        "rec_data": centred(keys[13], (SHOTS, STEPS, NREC), 1.0, 6.0, ((0, 16),), jnp.float32),
    }


second_coef = (-205.0 / 72.0, 8.0 / 5.0, -1.0 / 5.0, 8.0 / 315.0, -1.0 / 560.0)
first_coef = (0.8, -0.2, 4.0 / 105.0, -1.0 / 280.0)

def pad_axis(field, axis, width):
    widths = [(0, 0)] * field.ndim
    widths[axis] = (width, width)
    return jnp.pad(field, widths)

def shifted(padded, axis, offset, count):
    return lax.slice_in_dim(padded, 4 + offset, 4 + offset + count, axis=axis)

def second_along(padded, axis, count):
    result = second_coef[0] * shifted(padded, axis, 0, count)
    for offset in range(1, 5):
        result = result + second_coef[offset] * (shifted(padded, axis, offset, count) + shifted(padded, axis, -offset, count))
    return result

def first_along(padded, axis, count):
    result = first_coef[0] * (shifted(padded, axis, 1, count) - shifted(padded, axis, -1, count))
    for offset in range(2, 5):
        result = result + first_coef[offset - 1] * (shifted(padded, axis, offset, count) - shifted(padded, axis, -offset, count))
    return result

def apply_operator(padded_z, aniso_h, aniso_c):
    ndim = padded_z.ndim
    axis_x, axis_z, axis_y = (ndim - 3, ndim - 2, ndim - 1)
    count_z = padded_z.shape[axis_z] - 8
    count_x = padded_z.shape[axis_x]
    count_y = padded_z.shape[axis_y]
    centre = lax.slice_in_dim(padded_z, 4, 4 + count_z, axis=axis_z)
    depth_two = second_along(padded_z, axis_z, count_z)
    depth_one = first_along(padded_z, axis_z, count_z)
    lateral = second_along(pad_axis(centre, axis_x, 4), axis_x, count_x) + second_along(pad_axis(centre, axis_y, 4), axis_y, count_y)
    crossing = first_along(pad_axis(depth_one, axis_x, 4), axis_x, count_x)
    return aniso_h * lateral + depth_two + aniso_c * crossing

def relax_once(padded, centre, coef):
    neighbours = padded[2:, 1:-1, 1:-1] + padded[:-2, 1:-1, 1:-1]
    neighbours = neighbours + padded[1:-1, 2:, 1:-1] + padded[1:-1, :-2, 1:-1]
    neighbours = neighbours + padded[1:-1, 1:-1, 2:] + padded[1:-1, 1:-1, :-2]
    return centre + coef * (neighbours - 6.0 * centre)

def reference(u_prev, u_cur, a_prev, a_cur, model, aniso_h, aniso_c, smooth_coef, bin_onehot, shot_group, src_cell, rec_cell, src_wave, rec_data):
    cells = NX * NZ * NY
    powers = jnp.exp2(-jnp.arange(NBINS).astype(u_cur.dtype))
    block_weight = lax.optimization_barrier(jnp.sum(bin_onehot.astype(u_cur.dtype) * powers, axis=2))
    shot_weight = jnp.repeat(block_weight[shot_group], BZ, axis=1)

    def operate(field):
        return apply_operator(pad_axis(field, 1, 4), aniso_h, aniso_c)

    def one_shot(carry, items):
        older, wave, adj_old, adjoint, source, amplitude, receivers, records, weight = items
        gradient = jnp.zeros_like(wave)
        for step_index in range(STEPS):
            applied = operate(wave)
            adj_applied = operate(adjoint)
            gradient = gradient + adjoint * applied
            src_field = jnp.zeros((cells,), wave.dtype).at[source].add(amplitude[step_index]).reshape(NX, NZ, NY)
            rec_field = jnp.zeros((cells,), wave.dtype).at[receivers].add(records[step_index]).reshape(NX, NZ, NY)
            next_wave = 2.0 * wave - older + model * applied + src_field
            next_adj = 2.0 * adjoint - adj_old + model * adj_applied + rec_field
            older, wave = (wave, next_wave)
            adj_old, adjoint = (adjoint, next_adj)
        carry = carry + weight[None, :, None] * gradient
        return (carry, (older, wave))
    summed, (earlier, latest) = lax.scan(one_shot, jnp.zeros((NX, NZ, NY), u_cur.dtype), (u_prev, u_cur, a_prev, a_cur, src_cell, src_wave, rec_cell, rec_data, shot_weight))
    smoothed = summed
    for sweep_index in range(2):
        smoothed = relax_once(jnp.pad(smoothed, 1), smoothed, smooth_coef)
    square_sum = jnp.sum(smoothed * smoothed)
    norm_scale = jnp.sqrt(square_sum / (NX * NZ * NY) + 1e-06)
    grad_dir = smoothed / norm_scale
    model_next = model * (1.0 - 0.25 * jnp.tanh(grad_dir))

    def final_step(items):
        older, wave, source, amplitude = items
        src_field = jnp.zeros((cells,), wave.dtype).at[source].add(amplitude[STEPS]).reshape(NX, NZ, NY)
        applied = apply_operator(pad_axis(wave, 1, 4), aniso_h, aniso_c)
        return 2.0 * wave - older + model_next * applied + src_field
    wave_next = lax.map(final_step, (earlier, latest, src_cell, src_wave))
    return (model_next, grad_dir, wave_next)
```

```python
import functools

import jax
import jax.numpy as jnp
from jax import lax
from jax.experimental import pallas as pl
from jax.experimental.pallas import tpu as pltpu
from jax.sharding import PartitionSpec as P

MESH = pl.DeviceIdType.MESH
second_coef = (-205.0 / 72.0, 8.0 / 5.0, -1.0 / 5.0, 8.0 / 315.0, -1.0 / 560.0)
first_coef = (0.8, -0.2, 4.0 / 105.0, -1.0 / 280.0)
XP = 4
ZP = 8


def kernel(
    dims,
    u_prev,
    u_cur,
    a_prev,
    a_cur,
    model,
    aniso_h,
    aniso_c,
    smooth_coef,
    bins,
    shot_group,
    src_cell,
    rec_cell,
    src_wave,
    rec_data,
    model_next,
    grad_dir,
    wave_next,
    eu0,
    eu1,
    eu2,
    ea0,
    up,
    ap,
    coefs,
    eco,
    lat_u,
    dz_u,
    cr_u,
    lat_a,
    dz_a,
    cr_a,
    rec_field,
    a1,
    grad,
    half_in,
    part,
    block_in,
    es0,
    es1,
    sq,
    model_own,
    grad_own,
    load_sem,
    halo_send,
    halo_recv,
    g_send,
    g_recv,
    k_send,
    k_recv,
    s_send,
    s_recv,
    half_send,
    half_recv,
    rs_send,
    rs_recv,
    sq_send,
    sq_recv,
    out_sem,
):
    S, D, R, X, Z, Y, NB, BK = dims
    Q = S // 2
    O = Q // 2
    me = lax.axis_index("shot")
    d = lax.axis_index("depth")
    core = lax.rem(me, 2)
    chip = me // 2
    inner = lax.rem(chip, 2)
    outer = chip // 2
    ZI = slice(ZP, ZP + Z)

    def sid(o, p, c):
        return (o * 2 + p) * 2 + c

    own = pl.ds(me * R, R)
    loads = [
        pltpu.make_async_copy(model, coefs.at[0, own], load_sem.at[0]),
        pltpu.make_async_copy(aniso_h, coefs.at[1, own], load_sem.at[1]),
        pltpu.make_async_copy(aniso_c, coefs.at[2, own], load_sem.at[2]),
        pltpu.make_async_copy(smooth_coef, eco.at[own, ZI], load_sem.at[3]),
        pltpu.make_async_copy(u_cur.at[0], eu0.at[pl.ds(XP, X), ZI], load_sem.at[4]),
        pltpu.make_async_copy(a_cur.at[0], ea0.at[pl.ds(XP, X), ZI], load_sem.at[5]),
        pltpu.make_async_copy(u_prev.at[0], up, load_sem.at[6]),
        pltpu.make_async_copy(a_prev.at[0], ap, load_sem.at[7]),
    ]
    for load in loads:
        load.start()

    def zero_z(i, carry):
        for ref in (eu0, eu1, eu2, ea0, es0, es1):
            ref[i, 0:ZP, :] = jnp.zeros((ZP, Y), jnp.float32)
            ref[i, ZP + Z :, :] = jnp.zeros((ZP, Y), jnp.float32)
        return carry

    lax.fori_loop(0, X + 2 * XP, zero_z, 0)

    def zero_c(i, carry):
        eco[i, 0:ZP, :] = jnp.zeros((ZP, Y), jnp.float32)
        eco[i, ZP + Z :, :] = jnp.zeros((ZP, Y), jnp.float32)
        return carry

    lax.fori_loop(0, X, zero_c, 0)
    for ref in (eu0, eu1, eu2, ea0, es0, es1):
        for i in list(range(XP)) + list(range(XP + X, X + 2 * XP)):
            ref[i, ZI, :] = jnp.zeros((Z, Y), jnp.float32)
    for ref in (cr_u, cr_a):
        for i in list(range(XP)) + list(range(XP + X, X + 2 * XP)):
            ref[i] = jnp.zeros((Z, Y), jnp.float32)

    barrier = pltpu.get_barrier_semaphore()
    peers = [(sid(outer, inner, 1 - core), d)]
    for i in range(1, Q):
        peers.append((lax.rem(chip + i, Q) * 2 + core, d))
    for i in range(1, D):
        peers.append((me, lax.rem(d + i, D)))
    for peer in peers:
        pl.semaphore_signal(barrier, inc=1, device_id=peer, device_id_type=MESH)
    pl.semaphore_wait(barrier, len(peers))

    def remote(src, dst, ss, rs, peer):
        return pltpu.make_async_remote_copy(
            src_ref=src, dst_ref=dst, send_sem=ss, recv_sem=rs, device_id=peer, device_id_type=MESH
        )

    class Gather:
        def __init__(self, at, send, recv):
            self.at, self.send, self.recv = at, send, recv
            self.sent = []

        def go(self, s, sem, peer):
            copy = remote(self.at(s), self.at(s), self.send.at[sem], self.recv.at[sem], peer)
            copy.start()
            self.sent.append(copy)

        def landed(self, s, sem):
            ref = self.at(s)
            remote(ref, ref, self.send.at[sem], self.recv.at[sem], (me, d)).wait_recv()

        def start(self):
            for i in range(1, O):
                self.go(me, i, (sid(lax.rem(outer + i, O), inner, core), d))
            self.go(me, O, (sid(outer, 1 - inner, core), d))
            self.go(me, 2 * O, (sid(outer, inner, 1 - core), d))

        def forward_outer(self):
            for i in range(1, O):
                s = sid(lax.rem(outer + O - i, O), inner, core)
                self.landed(s, i)
                self.go(s, O + i, (sid(outer, 1 - inner, core), d))
                self.go(s, 2 * O + i, (sid(outer, inner, 1 - core), d))

        def forward_inner(self):
            for i in range(O):
                s = sid(lax.rem(outer + O - i, O), 1 - inner, core)
                self.landed(s, O + i)
                self.go(s, 3 * O + i, (sid(outer, inner, 1 - core), d))

        def finish(self):
            for i in range(O):
                self.landed(sid(lax.rem(outer + O - i, O), inner, 1 - core), 2 * O + i)
            for i in range(O):
                self.landed(sid(lax.rem(outer + O - i, O), 1 - inner, 1 - core), 3 * O + i)

        def drain(self):
            for copy in self.sent:
                copy.wait_send()

    class Halo:
        def __init__(self, ref, width, slot, rows):
            self.up = remote(
                ref.at[rows, ZP + Z - width : ZP + Z], ref.at[rows, ZP - width : ZP],
                halo_send.at[slot], halo_recv.at[slot], (me, jnp.minimum(d + 1, D - 1)),
            )
            self.down = remote(
                ref.at[rows, ZP : ZP + width], ref.at[rows, ZP + Z : ZP + Z + width],
                halo_send.at[slot + 1], halo_recv.at[slot + 1], (me, jnp.maximum(d - 1, 0)),
            )

        def start(self):
            pl.when(d < D - 1)(lambda: self.up.start())
            pl.when(d > 0)(lambda: self.down.start())

        def wait(self):
            pl.when(d > 0)(lambda: self.up.wait_recv())
            pl.when(d < D - 1)(lambda: self.down.wait_recv())

        def drain(self):
            pl.when(d < D - 1)(lambda: self.up.wait_send())
            pl.when(d > 0)(lambda: self.down.wait_send())

    rows = pl.ds(XP, X)
    for load in loads[:3]:
        load.wait()
    gather = Gather(lambda s: coefs.at[:, pl.ds(s * R, R)], g_send, g_recv)
    gather.start()
    loads[4].wait()
    halo_u0 = Halo(eu0, 4, 0, rows)
    halo_u0.start()
    loads[5].wait()
    halo_a0 = Halo(ea0, 4, 2, rows)
    halo_a0.start()
    loads[3].wait()
    gather_k = Gather(lambda s: eco.at[pl.ds(s * R, R), ZI], k_send, k_recv)
    gather_k.start()

    lane = lax.broadcasted_iota(jnp.int32, (R, Z, Y), 2)
    local_x = lax.broadcasted_iota(jnp.int32, (R, Z, Y), 0)
    local_z = lax.broadcasted_iota(jnp.int32, (R, Z, Y), 1)
    row_base = local_x * (Z * D) + local_z + d * Z

    def shift_y(v, k):
        rolled = pltpu.roll(v, k % Y, 2)
        keep = lane >= k if k > 0 else lane < Y + k
        return jnp.where(keep, rolled, 0.0)

    def lateral(ref, out):
        def step(s, carry):
            x = s * R
            centre = ref[pl.ds(x + XP, R), ZI, :]
            total = (2.0 * second_coef[0]) * centre
            for k in range(1, 5):
                total = total + second_coef[k] * (
                    (ref[pl.ds(x + XP + k, R), ZI, :] + ref[pl.ds(x + XP - k, R), ZI, :])
                    + (shift_y(centre, k) + shift_y(centre, -k))
                )
            out[pl.ds(x, R)] = total
            return carry

        lax.fori_loop(0, S, step, 0)

    def vertical(ref, out, cross):
        def step(s, carry):
            x = s * R
            mid = pl.ds(x + XP, R)
            two = second_coef[0] * ref[mid, ZI, :]
            one = jnp.zeros_like(two)
            for k in range(1, 5):
                high = ref[mid, ZP + k : ZP + k + Z, :]
                low = ref[mid, ZP - k : ZP - k + Z, :]
                two = two + second_coef[k] * (high + low)
                one = one + first_coef[k - 1] * (high - low)
            out[pl.ds(x, R)] = two
            cross[mid] = one
            return carry

        lax.fori_loop(0, S, step, 0)

    def combine(s, lat, dz, cross):
        x = s * R
        here = pl.ds(x, R)
        total = jnp.zeros((R, Z, Y), jnp.float32)
        for k in range(1, 5):
            total = total + first_coef[k - 1] * (
                cross[pl.ds(x + XP + k, R)] - cross[pl.ds(x + XP - k, R)]
            )
        return coefs[1, here] * lat[here] + dz[here] + coefs[2, here] * total

    source_row = src_cell[0] // Y
    source_y = src_cell[0] - source_row * Y

    def source(s, n):
        hit = (row_base + s * (R * Z * D) == source_row) & (lane == source_y)
        return jnp.where(hit, src_wave[0, n], 0.0)

    lateral(eu0, lat_u)
    gather.forward_outer()
    lateral(ea0, lat_a)

    cells = rec_cell[...]
    rec_row = cells // Y
    rec_y = cells - rec_row * Y
    records = rec_data[0, 0:1, :]
    nrec = cells.shape[1]
    spread = (lax.broadcasted_iota(jnp.int32, (Y, nrec), 0) == rec_y).astype(jnp.float32)
    many = R * Z
    flat = lax.broadcasted_iota(jnp.int32, (many, nrec), 0)
    flat_row = (flat // Z) * (Z * D) + lax.rem(flat, Z) + d * Z

    def receivers(s, carry):
        plane = jnp.where(flat_row + s * (R * Z * D) == rec_row, records, 0.0)
        placed = lax.dot_general(
            plane, spread, (((1,), (1,)), ((), ())),
            precision=lax.Precision.HIGHEST, preferred_element_type=jnp.float32,
        )
        rec_field[pl.ds(s * R, R)] = placed.reshape(R, Z, Y)
        return carry

    lax.fori_loop(0, S, receivers, 0)
    gather.forward_inner()
    halo_u0.wait()
    vertical(eu0, dz_u, cr_u)
    halo_a0.wait()
    vertical(ea0, dz_a, cr_a)
    loads[6].wait()
    loads[7].wait()
    gather.finish()

    def first_u(s, carry):
        here, mid = pl.ds(s * R, R), pl.ds(s * R + XP, R)
        applied = combine(s, lat_u, dz_u, cr_u)
        grad[s // 2, lax.rem(s, 2)] = ea0[mid, ZI, :] * applied
        eu1[mid, ZI, :] = 2.0 * eu0[mid, ZI, :] - up[here] + coefs[0, here] * applied + source(s, 0)
        return carry

    lax.fori_loop(0, S, first_u, 0)
    halo_u1 = Halo(eu1, 4, 4, rows)
    halo_u1.start()
    gather_k.forward_outer()

    def first_a(s, carry):
        here, mid = pl.ds(s * R, R), pl.ds(s * R + XP, R)
        applied = combine(s, lat_a, dz_a, cr_a)
        a1[here] = 2.0 * ea0[mid, ZI, :] - ap[here] + coefs[0, here] * applied + rec_field[here]
        return carry

    lax.fori_loop(0, S, first_a, 0)
    lateral(eu1, lat_u)
    gather_k.forward_inner()
    halo_u1.wait()
    vertical(eu1, dz_u, cr_u)

    group = shot_group[0]
    weight = jnp.zeros((R, Z, Y), jnp.float32)
    for block in range(BK):
        level = jnp.float32(0.0)
        for b in range(NB):
            level = level + bins[group, block, b].astype(jnp.float32) * (2.0 ** (-b))
        weight = jnp.where(local_z // (Z // BK) == block, level, weight)

    def second_u(s, carry):
        here, mid = pl.ds(s * R, R), pl.ds(s * R + XP, R)
        applied = combine(s, lat_u, dz_u, cr_u)
        q, c = s // 2, lax.rem(s, 2)
        grad[q, c] = weight * (grad[q, c] + a1[here] * applied)
        eu2[mid, ZI, :] = (
            2.0 * eu1[mid, ZI, :] - eu0[mid, ZI, :] + coefs[0, here] * applied + source(s, 1)
        )
        return carry

    lax.fori_loop(0, S, second_u, 0)
    half = remote(
        grad.at[:, 1 - core], half_in, half_send, half_recv, (sid(outer, inner, 1 - core), d)
    )
    half.start()
    halo_u2 = Halo(eu2, 4, 6, rows)
    halo_u2.start()
    gather_k.finish()
    halo_k = Halo(eco, 1, 8, pl.ds(0, X))
    halo_k.start()

    half.wait_recv()

    def add_half(q, carry):
        part[q] = grad[q, core] + half_in[q]
        return carry

    lax.fori_loop(0, Q, add_half, 0)
    scatter = []
    for i in range(1, Q):
        target = lax.rem(chip + i, Q)
        copy = remote(
            part.at[target], block_in.at[i - 1], rs_send.at[i - 1], rs_recv.at[i - 1],
            (target * 2 + core, d),
        )
        copy.start()
        scatter.append(copy)

    lateral(eu2, lat_a)
    for copy in scatter:
        copy.wait_recv()
    total = part[chip]
    for i in range(1, Q):
        total = total + block_in[i - 1]
    es0[pl.ds(me * R + XP, R), ZI, :] = total
    gather_s = Gather(lambda s: es0.at[pl.ds(s * R + XP, R), ZI], s_send, s_recv)
    gather_s.start()
    halo_u2.wait()
    vertical(eu2, dz_u, cr_u)
    gather_s.forward_outer()

    def final_u(s, carry):
        here, mid = pl.ds(s * R, R), pl.ds(s * R + XP, R)
        lat_u[here] = coefs[0, here] * combine(s, lat_a, dz_u, cr_u)
        up[here] = 2.0 * eu2[mid, ZI, :] - eu1[mid, ZI, :] + source(s, 2)
        return carry

    lax.fori_loop(0, S, final_u, 0)
    gather_s.forward_inner()
    gather_s.finish()
    halo_s = Halo(es0, 2, 10, rows)
    halo_s.start()
    halo_k.wait()
    halo_s.wait()

    def relax(src, s, z0, count):
        mid = pl.ds(s * R + XP, R)
        centre = src[mid, z0 : z0 + count, :]
        ln = lax.broadcasted_iota(jnp.int32, centre.shape, 2)
        around = src[pl.ds(s * R + XP + 1, R), z0 : z0 + count, :]
        around = around + src[pl.ds(s * R + XP - 1, R), z0 : z0 + count, :]
        around = around + src[mid, z0 + 1 : z0 + 1 + count, :] + src[mid, z0 - 1 : z0 - 1 + count, :]
        around = around + jnp.where(ln >= 1, pltpu.roll(centre, 1, 2), 0.0)
        around = around + jnp.where(ln < Y - 1, pltpu.roll(centre, Y - 1, 2), 0.0)
        return centre + eco[pl.ds(s * R, R), z0 : z0 + count, :] * (around - 6.0 * centre)

    def sweep_one(s, carry):
        es1[pl.ds(s * R + XP, R), ZP - 4 : ZP + Z + 4, :] = relax(es0, s, ZP - 4, Z + 8)
        return carry

    lax.fori_loop(0, S, sweep_one, 0)

    def sweep_two(s, squares):
        smoothed = relax(es1, s, ZP, Z)
        lat_a[pl.ds(s * R, R)] = smoothed
        return squares + jnp.sum(smoothed * smoothed, axis=0)

    squares = lax.fori_loop(0, S, sweep_two, jnp.zeros((Z, Y), jnp.float32))
    sq[0] = squares
    sums = []
    for i in range(1, D):
        copy = remote(
            sq.at[0], sq.at[i], sq_send.at[i - 1], sq_recv.at[i - 1], (me, lax.rem(d + i, D))
        )
        copy.start()
        sums.append(copy)
    for copy in sums:
        copy.wait_recv()
    for i in range(1, D):
        squares = squares + sq[i]
    mean = jnp.sum(squares) * (1.0 / (X * Z * D * Y))
    inverse = lax.rsqrt(jnp.full((R, Z, Y), mean + 1e-06, jnp.float32))

    def final(s, carry):
        here = pl.ds(s * R, R)
        wave = up[here] + lat_u[here] * (1.0 - 0.25 * jnp.tanh(lat_a[here] * inverse))
        dz_a[here] = wave
        return carry

    lax.fori_loop(0, S, final, 0)
    direction = lat_a[own] * inverse
    grad_own[...] = direction
    model_own[...] = coefs[0, own] * (1.0 - 0.25 * jnp.tanh(direction))
    outs = [
        pltpu.make_async_copy(dz_a, wave_next.at[0], out_sem.at[0]),
        pltpu.make_async_copy(model_own, model_next, out_sem.at[1]),
        pltpu.make_async_copy(grad_own, grad_dir, out_sem.at[2]),
    ]
    for copy in outs:
        copy.start()
    for one in (gather, gather_k, gather_s, halo_u0, halo_a0, halo_u1, halo_u2, halo_k, halo_s):
        one.drain()
    half.wait_send()
    for copy in scatter + sums:
        copy.wait_send()
    for copy in outs:
        copy.wait()


def solution(mesh):
    S, D = mesh.shape["shot"], mesh.shape["depth"]
    Q, O = S // 2, S // 4

    def body(u_prev, u_cur, a_prev, a_cur, model, *rest):
        _, X, Z, Y = u_cur.shape
        R = model.shape[0]
        bins = rest[3]
        dims = (S, D, R, X, Z, Y, bins.shape[2], bins.shape[1])
        f32 = jnp.float32
        field = pltpu.VMEM((X, Z, Y), f32)
        extended = pltpu.VMEM((X + 2 * XP, Z + 2 * ZP, Y), f32)
        crossing = pltpu.VMEM((X + 2 * XP, Z, Y), f32)
        dma = pltpu.SemaphoreType.DMA
        hbm = pl.BlockSpec(memory_space=pl.ANY)
        smem = pl.BlockSpec(memory_space=pltpu.SMEM)
        vmem = pl.BlockSpec(memory_space=pltpu.VMEM)
        return pl.pallas_call(
            functools.partial(kernel, dims),
            out_shape=(
                jax.ShapeDtypeStruct(model.shape, f32),
                jax.ShapeDtypeStruct(model.shape, f32),
                jax.ShapeDtypeStruct(u_cur.shape, f32),
            ),
            in_specs=[hbm] * 8 + [smem, smem, smem, vmem, smem, vmem],
            out_specs=[hbm] * 3,
            scratch_shapes=[
                extended,
                extended,
                extended,
                extended,
                field,
                field,
                pltpu.VMEM((3, X, Z, Y), f32),
                pltpu.VMEM((X, Z + 2 * ZP, Y), f32),
                field,
                field,
                crossing,
                field,
                field,
                crossing,
                field,
                field,
                pltpu.VMEM((Q, 2, R, Z, Y), f32),
                pltpu.VMEM((Q, R, Z, Y), f32),
                pltpu.VMEM((Q, R, Z, Y), f32),
                pltpu.VMEM((Q - 1, R, Z, Y), f32),
                extended,
                extended,
                pltpu.VMEM((D, Z, Y), f32),
                pltpu.VMEM((R, Z, Y), f32),
                pltpu.VMEM((R, Z, Y), f32),
                dma((8,)),
                dma((12,)),
                dma((12,)),
                dma((4 * O,)),
                dma((4 * O,)),
                dma((4 * O,)),
                dma((4 * O,)),
                dma((4 * O,)),
                dma((4 * O,)),
                dma,
                dma,
                dma((Q - 1,)),
                dma((Q - 1,)),
                dma((D - 1,)),
                dma((D - 1,)),
                dma((3,)),
            ],
            compiler_params=pltpu.CompilerParams(
                collective_id=0, has_side_effects=True, vmem_limit_bytes=40 * 1024 * 1024
            ),
        )(u_prev, u_cur, a_prev, a_cur, model, *rest)

    return jax.shard_map(
        body,
        mesh=mesh,
        in_specs=(P("shot", None, "depth", None),) * 4
        + (P("shot", "depth", None),) * 4
        + (
            P(None, "depth", None),
            P("shot"),
            P("shot"),
            P("shot", None),
            P("shot", None),
            P("shot", None, None),
        ),
        out_specs=(
            P("shot", "depth", None),
            P("shot", "depth", None),
            P("shot", None, "depth", None),
        ),
        check_vma=False,
    )
```

```python
import functools

import jax
import jax.numpy as jnp
from jax import lax
from jax.experimental import pallas as pl
from jax.experimental.pallas import tpu as pltpu
from jax.sharding import PartitionSpec as P

MESH = pl.DeviceIdType.MESH
second_coef = (-205.0 / 72.0, 8.0 / 5.0, -1.0 / 5.0, 8.0 / 315.0, -1.0 / 560.0)
first_coef = (0.8, -0.2, 4.0 / 105.0, -1.0 / 280.0)
XP = 4
ZP = 8


def kernel(
    dims,
    u_prev,
    u_cur,
    a_prev,
    a_cur,
    model,
    aniso_h,
    aniso_c,
    smooth_coef,
    bins,
    shot_group,
    src_cell,
    rec_cell,
    src_wave,
    rec_data,
    model_next,
    grad_dir,
    wave_next,
    eu0,
    eu1,
    eu2,
    ea0,
    up,
    ap,
    coefs,
    ec,
    band,
    lat_u,
    dz_u,
    cr_u,
    lat_a,
    dz_a,
    cr_a,
    rec_field,
    a1,
    grad,
    half_in,
    part,
    block_in,
    eb,
    eb1,
    smooth,
    sqd,
    sqs,
    load_sem,
    halo_send,
    halo_recv,
    g_send,
    g_recv,
    rim_send,
    rim_recv,
    s_send,
    s_recv,
    half_send,
    half_recv,
    rs_send,
    rs_recv,
    sqd_send,
    sqd_recv,
    sqs_send,
    sqs_recv,
):
    S, D, R, X, Z, Y, NB, BK = dims
    Q = S // 2
    O = Q // 2
    me = lax.axis_index("shot")
    d = lax.axis_index("depth")
    core = lax.rem(me, 2)
    chip = me // 2
    inner = lax.rem(chip, 2)
    outer = chip // 2
    ZI = slice(ZP, ZP + Z)

    def sid(o, p, c):
        return (o * 2 + p) * 2 + c

    own = pl.ds(me * R, R)
    loads = [
        pltpu.make_async_copy(model, coefs.at[0, own], load_sem.at[0]),
        pltpu.make_async_copy(aniso_h, coefs.at[1, own], load_sem.at[1]),
        pltpu.make_async_copy(aniso_c, coefs.at[2, own], load_sem.at[2]),
        pltpu.make_async_copy(smooth_coef, ec.at[pl.ds(2, R), ZI], load_sem.at[3]),
        pltpu.make_async_copy(u_cur.at[0], eu0.at[pl.ds(XP, X), ZI], load_sem.at[4]),
        pltpu.make_async_copy(a_cur.at[0], ea0.at[pl.ds(XP, X), ZI], load_sem.at[5]),
        pltpu.make_async_copy(u_prev.at[0], up, load_sem.at[6]),
        pltpu.make_async_copy(a_prev.at[0], ap, load_sem.at[7]),
    ]
    for load in loads:
        load.start()

    def zero_z(i, carry):
        for ref in (eu0, eu1, eu2, ea0):
            ref[i, 0:ZP, :] = jnp.zeros((ZP, Y), jnp.float32)
            ref[i, ZP + Z :, :] = jnp.zeros((ZP, Y), jnp.float32)
        return carry

    lax.fori_loop(0, X + 2 * XP, zero_z, 0)

    tall = jnp.zeros((2, Z + 2 * ZP, Y), jnp.float32)
    side = jnp.zeros((R, ZP, Y), jnp.float32)
    for ref in (eb, ec):
        ref[0:2] = tall
        ref[R + 2 : R + 4] = tall
        ref[2 : R + 2, 0:ZP, :] = side
        ref[2 : R + 2, ZP + Z :, :] = side

    for ref in (eu0, eu1, eu2, ea0):
        for i in list(range(XP)) + list(range(XP + X, X + 2 * XP)):
            ref[i, ZI, :] = jnp.zeros((Z, Y), jnp.float32)
    for ref in (cr_u, cr_a):
        for i in list(range(XP)) + list(range(XP + X, X + 2 * XP)):
            ref[i] = jnp.zeros((Z, Y), jnp.float32)

    barrier = pltpu.get_barrier_semaphore()
    peers = [(lax.rem(me + i, S), d) for i in range(1, S)]
    peers += [(me, lax.rem(d + i, D)) for i in range(1, D)]
    for dz in sorted({1, D - 1}):
        for dx in (1, S - 1):
            peers.append((lax.rem(me + dx, S), lax.rem(d + dz, D)))
    for peer in peers:
        pl.semaphore_signal(barrier, inc=1, device_id=peer, device_id_type=MESH)
    pl.semaphore_wait(barrier, len(peers))

    def remote(src, dst, ss, rs, peer):
        return pltpu.make_async_remote_copy(
            src_ref=src, dst_ref=dst, send_sem=ss, recv_sem=rs, device_id=peer, device_id_type=MESH
        )

    class Gather:
        def __init__(self, at, send, recv):
            self.at, self.send, self.recv = at, send, recv
            self.sent = []

        def go(self, s, sem, peer):
            copy = remote(self.at(s), self.at(s), self.send.at[sem], self.recv.at[sem], peer)
            copy.start()
            self.sent.append(copy)

        def landed(self, s, sem):
            ref = self.at(s)
            remote(ref, ref, self.send.at[sem], self.recv.at[sem], (me, d)).wait_recv()

        def start(self):
            for i in sorted(range(1, O), key=lambda i: min(i, O - i)):
                self.go(me, i, (sid(lax.rem(outer + i, O), inner, core), d))
            self.go(me, O, (sid(outer, 1 - inner, core), d))
            self.go(me, 2 * O, (sid(outer, inner, 1 - core), d))

        def forward_outer(self):
            for i in range(1, O):
                s = sid(lax.rem(outer + O - i, O), inner, core)
                self.landed(s, i)
                self.go(s, O + i, (sid(outer, 1 - inner, core), d))
                self.go(s, 2 * O + i, (sid(outer, inner, 1 - core), d))

        def forward_inner(self):
            for i in range(O):
                s = sid(lax.rem(outer + O - i, O), 1 - inner, core)
                self.landed(s, O + i)
                self.go(s, 3 * O + i, (sid(outer, inner, 1 - core), d))

        def finish(self):
            for i in range(O):
                self.landed(sid(lax.rem(outer + O - i, O), inner, 1 - core), 2 * O + i)
            for i in range(O):
                self.landed(sid(lax.rem(outer + O - i, O), 1 - inner, 1 - core), 3 * O + i)

        def drain(self):
            for copy in self.sent:
                copy.wait_send()

    class Halo:
        def __init__(self, ref, width, slot, rows):
            self.up = remote(
                ref.at[rows, ZP + Z - width : ZP + Z], ref.at[rows, ZP - width : ZP],
                halo_send.at[slot], halo_recv.at[slot], (me, jnp.minimum(d + 1, D - 1)),
            )
            self.down = remote(
                ref.at[rows, ZP : ZP + width], ref.at[rows, ZP + Z : ZP + Z + width],
                halo_send.at[slot + 1], halo_recv.at[slot + 1], (me, jnp.maximum(d - 1, 0)),
            )

        def start(self):
            pl.when(d < D - 1)(lambda: self.up.start())
            pl.when(d > 0)(lambda: self.down.start())

        def wait(self):
            pl.when(d > 0)(lambda: self.up.wait_recv())
            pl.when(d < D - 1)(lambda: self.down.wait_recv())

        def drain(self):
            pl.when(d < D - 1)(lambda: self.up.wait_send())
            pl.when(d > 0)(lambda: self.down.wait_send())

    class Rim:
        def __init__(self, ref, slot):
            self.parts = []
            for dx in (-1, 0, 1):
                for dz in (-1, 0, 1):
                    if dx == 0 and dz == 0:
                        continue
                    n = slot + len(self.parts)
                    xs, xd = {-1: ((2, 2), (R + 2, 2)), 0: ((2, R), (2, R)), 1: ((R, 2), (0, 2))}[dx]
                    zs, zd = {
                        -1: ((ZP, 2), (ZP + Z, 2)), 0: ((ZP, Z), (ZP, Z)), 1: ((ZP + Z - 2, 2), (ZP - 2, 2))
                    }[dz]
                    ts, td = me + dx, d + dz
                    goes = (ts >= 0) & (ts < S) & (td >= 0) & (td < D)
                    fs, fd = me - dx, d - dz
                    comes = (fs >= 0) & (fs < S) & (fd >= 0) & (fd < D)
                    copy = remote(
                        ref.at[pl.ds(*xs), pl.ds(*zs)], ref.at[pl.ds(*xd), pl.ds(*zd)],
                        rim_send.at[n], rim_recv.at[n],
                        (jnp.clip(ts, 0, S - 1), jnp.clip(td, 0, D - 1)),
                    )
                    self.parts.append((copy, goes, comes))

        def start(self):
            for copy, goes, comes in self.parts:
                pl.when(goes)(copy.start)

        def wait(self):
            for copy, goes, comes in self.parts:
                pl.when(comes)(copy.wait_recv)

        def drain(self):
            for copy, goes, comes in self.parts:
                pl.when(goes)(copy.wait_send)

    rows = pl.ds(XP, X)
    for load in loads[:3]:
        load.wait()
    gather = Gather(lambda s: coefs.at[:, pl.ds(s * R, R)], g_send, g_recv)
    gather.start()
    loads[4].wait()
    halo_u0 = Halo(eu0, 4, 0, rows)
    halo_u0.start()
    loads[5].wait()
    halo_a0 = Halo(ea0, 4, 2, rows)
    halo_a0.start()
    loads[3].wait()
    rim_k = Rim(ec, 0)
    rim_k.start()

    lane = lax.broadcasted_iota(jnp.int32, (R, Z, Y), 2)
    local_x = lax.broadcasted_iota(jnp.int32, (R, Z, Y), 0)
    local_z = lax.broadcasted_iota(jnp.int32, (R, Z, Y), 1)
    row_base = local_x * (Z * D) + local_z + d * Z

    gap = lax.abs(
        lax.broadcasted_iota(jnp.int32, (Y, Y), 0) - lax.broadcasted_iota(jnp.int32, (Y, Y), 1)
    )
    exact = jnp.where(gap == 0, 2.0 * second_coef[0], 0.0)
    for k in range(1, 5):
        exact = jnp.where(gap == k, second_coef[k], exact)
    head = exact.astype(jnp.bfloat16)
    rest = (exact - head.astype(jnp.float32)).astype(jnp.bfloat16)
    band[0:Y, 0:Y] = head
    band[Y:, 0:Y] = head
    band[0:Y, Y:] = rest
    band[Y:, Y:] = jnp.zeros((Y, Y), jnp.bfloat16)

    def halves(v):
        top = v.astype(jnp.bfloat16)
        return jnp.concatenate([top, (v - top.astype(jnp.float32)).astype(jnp.bfloat16)], axis=-1)

    CH = 16 if X % 16 == 0 else R

    def lateral(ref, out):
        def step(i, carry):
            x = i * CH
            centre = ref[pl.ds(x + XP, CH), ZI, :].reshape(CH * Z, Y)
            both = jnp.dot(halves(centre), band[...], preferred_element_type=jnp.float32)
            total = (both[:, :Y] + both[:, Y:]).reshape(CH, Z, Y)
            for k in range(1, 5):
                total = total + second_coef[k] * (
                    ref[pl.ds(x + XP + k, CH), ZI, :] + ref[pl.ds(x + XP - k, CH), ZI, :]
                )
            out[pl.ds(x, CH)] = total
            return carry

        lax.fori_loop(0, X // CH, step, 0)

    def vertical(ref, out, cross):
        def step(s, carry):
            x = s * R
            mid = pl.ds(x + XP, R)
            two = second_coef[0] * ref[mid, ZI, :]
            one = jnp.zeros_like(two)
            for k in range(1, 5):
                high = ref[mid, ZP + k : ZP + k + Z, :]
                low = ref[mid, ZP - k : ZP - k + Z, :]
                two = two + second_coef[k] * (high + low)
                one = one + first_coef[k - 1] * (high - low)
            out[pl.ds(x, R)] = two
            cross[mid] = one
            return carry

        lax.fori_loop(0, S, step, 0)

    def combine(s, lat, dz, cross):
        x = s * R
        here = pl.ds(x, R)
        total = jnp.zeros((R, Z, Y), jnp.float32)
        for k in range(1, 5):
            total = total + first_coef[k - 1] * (
                cross[pl.ds(x + XP + k, R)] - cross[pl.ds(x + XP - k, R)]
            )
        return coefs[1, here] * lat[here] + dz[here] + coefs[2, here] * total

    source_row = src_cell[0] // Y
    source_y = src_cell[0] - source_row * Y

    def source(s, n):
        hit = (row_base + s * (R * Z * D) == source_row) & (lane == source_y)
        return jnp.where(hit, src_wave[0, n], 0.0)

    lateral(eu0, lat_u)
    gather.forward_outer()
    lateral(ea0, lat_a)

    cells = rec_cell[...]
    rec_row = cells // Y
    rec_y = cells - rec_row * Y
    records = rec_data[0, 0:1, :]
    nrec = cells.shape[1]
    spread = (lax.broadcasted_iota(jnp.int32, (Y, nrec), 0) == rec_y).astype(jnp.float32)
    spread = spread.astype(jnp.bfloat16)
    spread = jnp.concatenate([spread, spread], axis=1)
    many = CH * Z
    flat = lax.broadcasted_iota(jnp.int32, (many, nrec), 0)
    flat_row = (flat // Z) * (Z * D) + lax.rem(flat, Z) + d * Z

    def receivers(s, carry):
        plane = halves(jnp.where(flat_row + s * (CH * Z * D) == rec_row, records, 0.0))
        placed = lax.dot_general(
            plane, spread, (((1,), (1,)), ((), ())),
            preferred_element_type=jnp.float32,
        )
        rec_field[pl.ds(s * CH, CH)] = placed.reshape(CH, Z, Y)
        return carry

    lax.fori_loop(0, X // CH, receivers, 0)
    gather.forward_inner()
    halo_u0.wait()
    vertical(eu0, dz_u, cr_u)
    halo_a0.wait()
    vertical(ea0, dz_a, cr_a)
    loads[6].wait()
    loads[7].wait()
    gather.finish()

    def first_u(s, carry):
        here, mid = pl.ds(s * R, R), pl.ds(s * R + XP, R)
        applied = combine(s, lat_u, dz_u, cr_u)
        grad[s // 2, lax.rem(s, 2)] = ea0[mid, ZI, :] * applied
        eu1[mid, ZI, :] = 2.0 * eu0[mid, ZI, :] - up[here] + coefs[0, here] * applied + source(s, 0)
        return carry

    lax.fori_loop(0, S, first_u, 0)
    halo_u1 = Halo(eu1, 4, 4, rows)
    halo_u1.start()

    def first_a(s, carry):
        here, mid = pl.ds(s * R, R), pl.ds(s * R + XP, R)
        applied = combine(s, lat_a, dz_a, cr_a)
        a1[here] = 2.0 * ea0[mid, ZI, :] - ap[here] + coefs[0, here] * applied + rec_field[here]
        return carry

    lax.fori_loop(0, S, first_a, 0)
    lateral(eu1, lat_u)
    halo_u1.wait()
    vertical(eu1, dz_u, cr_u)

    group = shot_group[0]
    marks = bins[group].astype(jnp.float32)
    power = lax.broadcasted_iota(jnp.int32, (BK, NB), 1)
    scale = jnp.zeros((BK, NB), jnp.float32)
    for b in range(NB):
        scale = jnp.where(power == b, 2.0 ** (-b), scale)
    levels = jnp.sum(marks * scale, axis=1, keepdims=True)
    weight = jnp.zeros((R, Z, Y), jnp.float32)
    for block in range(BK):
        weight = jnp.where(local_z // (Z // BK) == block, levels[block : block + 1, 0:1], weight)

    def second_u(s, carry):
        here, mid = pl.ds(s * R, R), pl.ds(s * R + XP, R)
        applied = combine(s, lat_u, dz_u, cr_u)
        q, c = s // 2, lax.rem(s, 2)
        grad[q, c] = weight * (grad[q, c] + a1[here] * applied)
        eu2[mid, ZI, :] = (
            2.0 * eu1[mid, ZI, :] - eu0[mid, ZI, :] + coefs[0, here] * applied + source(s, 1)
        )
        return carry

    lax.fori_loop(0, S, second_u, 0)
    half = remote(
        grad.at[:, 1 - core], half_in, half_send, half_recv, (sid(outer, inner, 1 - core), d)
    )
    half.start()
    halo_u2 = Halo(eu2, 4, 6, rows)
    halo_u2.start()

    half.wait_recv()

    def add_half(q, carry):
        part[q] = grad[q, core] + half_in[q]
        return carry

    lax.fori_loop(0, Q, add_half, 0)
    scatter = []
    for i in range(1, Q):
        target = lax.rem(chip + i, Q)
        copy = remote(
            part.at[target], block_in.at[i - 1], rs_send.at[i - 1], rs_recv.at[i - 1],
            (target * 2 + core, d),
        )
        copy.start()
        scatter.append(copy)

    lateral(eu2, lat_a)
    for copy in scatter:
        copy.wait_recv()
    total = part[chip]
    for i in range(1, Q):
        total = total + block_in[i - 1]
    eb[2 : R + 2, ZI, :] = total
    rim_s = Rim(eb, 8)
    rim_s.start()
    rim_k.wait()
    halo_u2.wait()
    vertical(eu2, dz_u, cr_u)
    rim_s.wait()

    def relax(src, x0, nx, z0, count):
        centre = src[x0 : x0 + nx, z0 : z0 + count, :]
        ln = lax.broadcasted_iota(jnp.int32, centre.shape, 2)
        around = src[x0 + 1 : x0 + 1 + nx, z0 : z0 + count, :]
        around = around + src[x0 - 1 : x0 - 1 + nx, z0 : z0 + count, :]
        around = around + src[x0 : x0 + nx, z0 + 1 : z0 + 1 + count, :]
        around = around + src[x0 : x0 + nx, z0 - 1 : z0 - 1 + count, :]
        around = around + jnp.where(ln >= 1, pltpu.roll(centre, 1, 2), 0.0)
        around = around + jnp.where(ln < Y - 1, pltpu.roll(centre, Y - 1, 2), 0.0)
        return centre + ec[x0 : x0 + nx, z0 : z0 + count, :] * (around - 6.0 * centre)

    eb1[1 : R + 3, ZP - 4 : ZP + Z + 4, :] = relax(eb, 1, R + 2, ZP - 4, Z + 8)
    smoothed = relax(eb1, 2, R, ZP, Z)
    smooth[own] = smoothed
    gather_s = Gather(lambda s: smooth.at[pl.ds(s * R, R)], s_send, s_recv)
    gather_s.start()
    squares = jnp.sum((smoothed * smoothed).reshape(R * Z // 8, 8, Y), axis=0)
    sqd[0] = squares
    sums = []
    for i in range(1, D):
        copy = remote(
            sqd.at[0], sqd.at[i], sqd_send.at[i - 1], sqd_recv.at[i - 1], (me, lax.rem(d + i, D))
        )
        copy.start()
        sums.append(copy)
    for copy in sums:
        copy.wait_recv()
    for i in range(1, D):
        squares = squares + sqd[i]
    sqs[0] = squares
    slab = []
    for i in range(1, S):
        copy = remote(
            sqs.at[0], sqs.at[i], sqs_send.at[i - 1], sqs_recv.at[i - 1], (lax.rem(me + i, S), d)
        )
        copy.start()
        slab.append(copy)
    gather_s.forward_outer()

    def final_u(s, carry):
        here, mid = pl.ds(s * R, R), pl.ds(s * R + XP, R)
        lat_u[here] = coefs[0, here] * combine(s, lat_a, dz_u, cr_u)
        up[here] = 2.0 * eu2[mid, ZI, :] - eu1[mid, ZI, :] + source(s, 2)
        return carry

    lax.fori_loop(0, S, final_u, 0)
    gather_s.forward_inner()
    for copy in slab:
        copy.wait_recv()
    for i in range(1, S):
        squares = squares + sqs[i]
    mean = jnp.sum(squares) * (1.0 / (X * Z * D * Y))
    inverse = lax.rsqrt(jnp.full((R, Z, Y), mean + 1e-06, jnp.float32))
    direction = smoothed * inverse
    grad_dir[...] = direction
    model_next[...] = coefs[0, own] * (1.0 - 0.25 * jnp.tanh(direction))
    gather_s.finish()

    def final(s, carry):
        here = pl.ds(s * R, R)
        wave_next[0, here] = up[here] + lat_u[here] * (1.0 - 0.25 * jnp.tanh(smooth[here] * inverse))
        return carry

    lax.fori_loop(0, S, final, 0)
    for one in (gather, gather_s, halo_u0, halo_a0, halo_u1, halo_u2, rim_k, rim_s):
        one.drain()
    half.wait_send()
    for copy in scatter + sums + slab:
        copy.wait_send()


def solution(mesh):
    S, D = mesh.shape["shot"], mesh.shape["depth"]
    Q, O = S // 2, S // 4

    def body(u_prev, u_cur, a_prev, a_cur, model, *rest):
        _, X, Z, Y = u_cur.shape
        R = model.shape[0]
        bins = rest[3]
        dims = (S, D, R, X, Z, Y, bins.shape[2], bins.shape[1])
        f32 = jnp.float32
        field = pltpu.VMEM((X, Z, Y), f32)
        extended = pltpu.VMEM((X + 2 * XP, Z + 2 * ZP, Y), f32)
        crossing = pltpu.VMEM((X + 2 * XP, Z, Y), f32)
        dma = pltpu.SemaphoreType.DMA
        hbm = pl.BlockSpec(memory_space=pltpu.HBM)
        smem = pl.BlockSpec(memory_space=pltpu.SMEM)
        vmem = pl.BlockSpec(memory_space=pltpu.VMEM)
        return pl.pallas_call(
            functools.partial(kernel, dims),
            out_shape=(
                jax.ShapeDtypeStruct(model.shape, f32),
                jax.ShapeDtypeStruct(model.shape, f32),
                jax.ShapeDtypeStruct(u_cur.shape, f32),
            ),
            in_specs=[hbm] * 8 + [vmem, smem, smem, vmem, smem, vmem],
            out_specs=[vmem] * 3,
            scratch_shapes=[
                extended,
                extended,
                extended,
                extended,
                field,
                field,
                pltpu.VMEM((3, X, Z, Y), f32),
                pltpu.VMEM((R + 4, Z + 2 * ZP, Y), f32),
                pltpu.VMEM((2 * Y, 2 * Y), jnp.bfloat16),
                field,
                field,
                crossing,
                field,
                field,
                crossing,
                field,
                field,
                pltpu.VMEM((Q, 2, R, Z, Y), f32),
                pltpu.VMEM((Q, R, Z, Y), f32),
                pltpu.VMEM((Q, R, Z, Y), f32),
                pltpu.VMEM((Q - 1, R, Z, Y), f32),
                pltpu.VMEM((R + 4, Z + 2 * ZP, Y), f32),
                pltpu.VMEM((R + 4, Z + 2 * ZP, Y), f32),
                field,
                pltpu.VMEM((D, 8, Y), f32),
                pltpu.VMEM((S, 8, Y), f32),
                dma((8,)),
                dma((8,)),
                dma((8,)),
                dma((4 * O,)),
                dma((4 * O,)),
                dma((16,)),
                dma((16,)),
                dma((4 * O,)),
                dma((4 * O,)),
                dma,
                dma,
                dma((Q - 1,)),
                dma((Q - 1,)),
                dma((D - 1,)),
                dma((D - 1,)),
                dma((S - 1,)),
                dma((S - 1,)),
            ],
            compiler_params=pltpu.CompilerParams(
                collective_id=0, has_side_effects=True, vmem_limit_bytes=56 * 1024 * 1024
            ),
        )(u_prev, u_cur, a_prev, a_cur, model, *rest)

    return jax.shard_map(
        body,
        mesh=mesh,
        in_specs=(P("shot", None, "depth", None),) * 4
        + (P("shot", "depth", None),) * 4
        + (
            P(None, "depth", None),
            P("shot"),
            P("shot"),
            P("shot", None),
            P("shot", None),
            P("shot", None, None),
        ),
        out_specs=(
            P("shot", "depth", None),
            P("shot", "depth", None),
            P("shot", None, "depth", None),
        ),
        check_vma=False,
    )
```
